32 devices in a mesh: frames: 32 (over z, y, x, core), centers: 1.
Axes of the slice: x: 2, y: 2, z: 4, core: 2. Of those that a mesh axis runs over, the one named last changes fastest.
Arguments:
- frames: bfloat16 [32768, 512], P('frames'), may hold values from -24 to 24
- centers: bfloat16 [16384, 512], P('centers'), may hold values from -6 to 6
- starts: int32 [64], replicated, may hold values from 0 to 32767, as said below
Outputs:
- counts: float32 [512, 16384], P('frames', 'centers')
The draws below stay inside these ranges and needn't reach their ends.
Inputs may be any that keep to these rules, and one draw needn't show every extreme that they name: starts[0] is 0 and the entries rise strictly.
All inputs are finite; a program needn't handle non-finite values.
Results may differ from the reference program's by a relative error of at most 0.001.
Values may be sent and summed in bfloat16 or wider, within the bound.
A program may use at most 192 MiB of HBM per device.

```python
import jax
import jax.numpy as jnp
from jax import lax

D = 512
K = 16384
W = 512
LAG = 5
F_DEV = 1024
NSEG = 64
NF = 32768


def draw_frames(key, part):
    base = jax.random.normal(key, (NF, D), jnp.float32)
    base = jnp.clip(base, -6.0, 6.0)
    chosen = jax.random.uniform(jax.random.fold_in(key, 11), (NF, 1), jnp.float32) < 0.03125
    level = jax.random.randint(jax.random.fold_in(key, 13), (NF, 1), 0, 3).astype(jnp.float32)
    flip = jax.random.uniform(jax.random.fold_in(key, 17), (NF, 1), jnp.float32) < 0.5
    offset = (12.0 + 4.0 * level) * jnp.where(flip, -1.0, 1.0)
    base = jnp.clip(base + jnp.where(chosen, offset, 0.0), -24.0, 24.0)
    return base.astype(jnp.bfloat16)


def draw_starts(key, part):
    picks = jax.random.permutation(key, NF - 1)[:NSEG - 1] + 1
    return jnp.concatenate([jnp.zeros((1,), jnp.int32), jnp.sort(picks).astype(jnp.int32)])


def scatter_about(own_key, extent, width, limit, held_as=jnp.bfloat16):
    return jnp.clip(width * jax.random.normal(own_key, extent, jnp.float32), -limit, limit).astype(held_as)


def setup_inputs(seed: int = 0) -> dict:
    seeds = jax.random.split(jax.random.key(seed), 4)
    frames = draw_frames(jax.random.fold_in(seeds[3], 71), 0)
    centers = scatter_about(seeds[1], (K, D), 1.0, 6.0)
    starts = draw_starts(jax.random.fold_in(seeds[3], 71), 0)
    return {"frames": frames, "centers": centers, "starts": starts}


SHARPNESS = 0.03125


def logits_of(row_block, centers):
    inner_prod = jnp.dot(row_block, centers.T, preferred_element_type=jnp.float32)
    frame_norm = jnp.sum(row_block.astype(jnp.float32) ** 2, axis=1, keepdims=True)
    center_norm = jnp.sum(centers.astype(jnp.float32) ** 2, axis=1)
    return -SHARPNESS * (frame_norm - 2.0 * inner_prod + center_norm[None, :])


def segment_of(positions, starts):
    return jnp.sum((starts[None, :] <= positions[:, None]).astype(jnp.int32), axis=1)


def pair_mask(positions, starts):
    later = positions + LAG
    same = segment_of(positions, starts) == segment_of(later, starts)
    return jnp.logical_and(same, later < NF)


def reference(frames, centers, starts):
    padded = jnp.concatenate([frames, jnp.zeros((LAG, D), frames.dtype)], axis=0)

    def block(accumulated, block_index):
        first_frame = block_index * F_DEV
        row_block = lax.dynamic_slice_in_dim(padded, first_frame, F_DEV + LAG, 0)
        logits = logits_of(row_block, centers)
        row_top = jnp.max(logits, axis=1, keepdims=True)
        exponent = jnp.exp(logits - row_top)
        member = (exponent / jnp.sum(exponent, axis=1, keepdims=True)).astype(jnp.bfloat16)
        positions = first_frame + jnp.arange(F_DEV, dtype=jnp.int32)
        usable = pair_mask(positions, starts)
        lead_rows = member[:F_DEV, :W] * usable[:, None].astype(jnp.bfloat16)
        lag_rows = member[LAG:, :]
        partial_value = lax.dot_general(lead_rows, lag_rows, (((0,), (0,)), ((), ())), preferred_element_type=jnp.float32)
        return accumulated + partial_value, None

    counts, _ = lax.scan(block, jnp.zeros((W, K), jnp.float32), jnp.arange(NF // F_DEV, dtype=jnp.int32))
    return counts * (K * K / NF)
```

```python
import math

import jax
import jax.numpy as jnp
from jax import lax
from jax.experimental import pallas as pl
from jax.experimental.pallas import tpu as pltpu
from jax.sharding import PartitionSpec as P

K = 16384
W = 512
LAG = 5
GROUP = 8
HALO = 128
TAIL = 16
TILE = 512
SHARPNESS = 0.03125
ALPHA = 2.0 * SHARPNESS * math.log2(math.e)
VMEM_BYTES = 56 * 1024 * 1024
TRANS_B = (((1,), (1,)), ((), ()))


def weights_of(points, norms, rows):
    score = (
        lax.dot_general(points, rows, TRANS_B, preferred_element_type=jnp.float32) - norms
    )
    top = jnp.max(score, axis=0, keepdims=True)
    return top, jnp.exp2(ALPHA * (score - top))


def member_kernel(
    rows_ref, halo_ref, centers_ref, center_norm_ref, source_ref, source_norm_ref,
    member_ref, lead_ref, top_ref, sum_ref, lead_top_ref,
    halo_top_ref, halo_sum_ref, halo_lead_top_ref, carry_ref,
):
    step = pl.program_id(0)

    @pl.when(step == 0)
    def _():
        rows = halo_ref[...]
        top, weight = weights_of(centers_ref[...], center_norm_ref[...], rows)
        halo_top_ref[...] = top
        halo_sum_ref[...] = jnp.sum(weight, axis=0, keepdims=True)
        top, weight = weights_of(source_ref[...], source_norm_ref[...], rows)
        halo_lead_top_ref[...] = top
        carry_ref[...] = pltpu.roll(weight, LAG, 1)

    @pl.when(step > 0)
    def _():
        rows = rows_ref[...]
        top, weight = weights_of(centers_ref[...], center_norm_ref[...], rows)
        top_ref[...] = top
        sum_ref[...] = jnp.sum(weight, axis=0, keepdims=True)
        member_ref[...] = weight.astype(jnp.bfloat16)
        top, weight = weights_of(source_ref[...], source_norm_ref[...], rows)
        lead_top_ref[...] = top
        moved = pltpu.roll(weight, LAG, 1)
        lane = lax.broadcasted_iota(jnp.int32, (W, HALO), 1)
        first = moved[:, :HALO]
        lead_ref[:, :HALO] = jnp.where(lane < LAG, carry_ref[...], first).astype(jnp.bfloat16)
        lead_ref[:, HALO:] = moved[:, HALO:].astype(jnp.bfloat16)
        carry_ref[...] = first


def members(rows, halo, centers, center_norm, source, source_norm):
    frame_count, depth = rows.shape
    states = centers.shape[0]
    steps = frame_count // TILE
    whole = lambda i: (0, 0)
    along = lambda i: (0, jnp.maximum(i - 1, 0))
    stat = jax.ShapeDtypeStruct((1, frame_count), jnp.float32)
    halo_stat = jax.ShapeDtypeStruct((1, HALO), jnp.float32)
    return pl.pallas_call(
        member_kernel,
        grid=(steps + 1,),
        in_specs=[
            pl.BlockSpec((TILE, depth), lambda i: (jnp.maximum(i - 1, 0), 0)),
            pl.BlockSpec((HALO, depth), whole),
            pl.BlockSpec((states, depth), whole),
            pl.BlockSpec((states, 1), whole),
            pl.BlockSpec((W, depth), whole),
            pl.BlockSpec((W, 1), whole),
        ],
        out_specs=[
            pl.BlockSpec((states, TILE), along),
            pl.BlockSpec((W, TILE), along),
            pl.BlockSpec((1, TILE), along),
            pl.BlockSpec((1, TILE), along),
            pl.BlockSpec((1, TILE), along),
            pl.BlockSpec((1, HALO), whole),
            pl.BlockSpec((1, HALO), whole),
            pl.BlockSpec((1, HALO), whole),
        ],
        out_shape=[
            jax.ShapeDtypeStruct((states, frame_count), jnp.bfloat16),
            jax.ShapeDtypeStruct((W, frame_count), jnp.bfloat16),
            stat, stat, stat, halo_stat, halo_stat, halo_stat,
        ],
        scratch_shapes=[pltpu.VMEM((W, HALO), jnp.float32)],
        compiler_params=pltpu.CompilerParams(vmem_limit_bytes=VMEM_BYTES),
        cost_estimate=pl.CostEstimate(
            flops=2 * frame_count * depth * (states + W),
            bytes_accessed=2 * frame_count * (states + W + depth),
            transcendentals=frame_count * (states + W),
        ),
        name="members",
    )(rows, halo, centers, center_norm, source, source_norm)


def counts_kernel(lead_ref, scale_ref, member_ref, out_ref):
    @pl.when(pl.program_id(0) == 0)
    def _():
        out_ref[...] = jnp.zeros_like(out_ref)

    lead = (lead_ref[...].astype(jnp.float32) * scale_ref[...]).astype(jnp.bfloat16)
    out_ref[...] += lax.dot_general(
        lead, member_ref[...], TRANS_B, preferred_element_type=jnp.float32
    )


def counts_of(lead, scale, member):
    states, frame_count = member.shape
    tile = 2 * TILE
    return pl.pallas_call(
        counts_kernel,
        grid=(frame_count // tile,),
        in_specs=[
            pl.BlockSpec((W, tile), lambda i: (0, i)),
            pl.BlockSpec((1, tile), lambda i: (0, i)),
            pl.BlockSpec((states, tile), lambda i: (0, i)),
        ],
        out_specs=pl.BlockSpec((W, states), lambda i: (0, 0)),
        out_shape=jax.ShapeDtypeStruct((W, states), jnp.float32),
        compiler_params=pltpu.CompilerParams(vmem_limit_bytes=VMEM_BYTES),
        cost_estimate=pl.CostEstimate(
            flops=2 * frame_count * W * states,
            bytes_accessed=2 * frame_count * (states + W),
            transcendentals=0,
        ),
        name="counts",
    )(lead, scale, member)


def segment_of(positions, starts):
    return jnp.sum((starts[:, None] <= positions[None, :]).astype(jnp.int32), axis=0)


def half_norm(points):
    return 0.5 * jnp.sum(points.astype(jnp.float32) ** 2, axis=1, keepdims=True)


def shards(frames, centers, starts):
    device_frames, depth = frames.shape
    devices = lax.axis_size("frames")
    planes = devices // GROUP
    me = lax.axis_index("frames")
    plane, place = me // GROUP, me % GROUP
    groups = [[p * GROUP + c for c in range(GROUP)] for p in range(planes)]

    tails = lax.all_gather(frames[-TAIL:], "frames")
    rows = lax.all_gather(frames, "frames", axis_index_groups=groups, tiled=True)
    before = lax.dynamic_index_in_dim(
        tails, jnp.maximum(plane * GROUP - 1, 0), 0, keepdims=False
    )
    halo = jnp.concatenate([jnp.zeros((HALO - TAIL, depth), frames.dtype), before], axis=0)

    states = centers.shape[0] // GROUP
    own = lax.dynamic_slice_in_dim(centers, place * states, states, 0)
    source = centers[:W]
    if lax.axis_size("centers") > 1:
        mine = lax.axis_index("centers") == 0
        source = lax.psum(jnp.where(mine, source, jnp.zeros_like(source)), "centers")

    member, lead, top, total, lead_top, halo_top, halo_total, halo_lead_top = members(
        rows, halo, own, half_norm(own), source, half_norm(source)
    )

    stats = jnp.concatenate(
        [
            jnp.concatenate([halo_top, top], axis=1),
            jnp.concatenate([halo_total, total], axis=1),
        ],
        axis=0,
    )
    gathered = lax.all_gather(stats, "frames", axis_index_groups=groups)
    all_top = lax.pmax(jnp.max(gathered[:, 0], axis=0), "centers")
    all_total = lax.psum(
        jnp.sum(gathered[:, 1] * jnp.exp2(ALPHA * (gathered[:, 0] - all_top)), axis=0),
        "centers",
    )

    plane_frames = rows.shape[0]
    positions = plane * plane_frames - HALO + jnp.arange(plane_frames + HALO, dtype=jnp.int32)
    usable = jnp.logical_and(
        segment_of(positions, starts) == segment_of(positions + LAG, starts),
        jnp.logical_and(positions >= 0, positions + LAG < plane_frames * planes),
    )
    lead_tops = jnp.concatenate([halo_lead_top, lead_top], axis=1)[0]
    lead_factor = jnp.where(usable, jnp.exp2(ALPHA * (lead_tops - all_top)) / all_total, 0.0)
    lag_factor = jnp.exp2(ALPHA * (top[0] - all_top[HALO:])) / all_total[HALO:]
    scale = lead_factor[HALO - LAG : HALO - LAG + plane_frames] * lag_factor

    partial = counts_of(lead, scale[None, :], member)

    row_top = jnp.max(partial, axis=1, keepdims=True)
    power = jnp.clip(jnp.floor(jnp.log2(jnp.maximum(row_top, 1e-30))), -100.0, 100.0)
    scaled = (partial * jnp.exp2(14.0 - power)).astype(jnp.float16)
    sent = jnp.concatenate(
        [scaled, jnp.broadcast_to(power.astype(jnp.float16), (W, 128))], axis=1
    )
    owned = W // devices
    received = lax.all_to_all(
        sent.reshape(devices, owned, states + 128), "frames", split_axis=0, concat_axis=0, tiled=True
    ).astype(jnp.float32)
    unit = jnp.exp2(received[:, :, states : states + 1] - 14.0)
    summed = jnp.sum(
        (received[:, :, :states] * unit).reshape(planes, GROUP, owned, states), axis=0
    )
    summed = summed * (K * K / (plane_frames * planes))
    return summed.transpose(1, 0, 2).reshape(owned, GROUP * states)


def solution(mesh):
    return jax.shard_map(
        shards,
        mesh=mesh,
        in_specs=(P("frames", None), P("centers", None), P()),
        out_specs=P("frames", "centers"),
        check_vma=False,
    )
```

```python
import functools
import math

import jax
import jax.numpy as jnp
from jax import lax
from jax.experimental import pallas as pl
from jax.experimental.pallas import tpu as pltpu
from jax.sharding import PartitionSpec as P

K = 16384
W = 512
LAG = 5
GROUP = 8
HALO = 128
TAIL = 16
TILE = 512
SHARPNESS = 0.03125
ALPHA = 2.0 * SHARPNESS * math.log2(math.e)
VMEM_BYTES = 56 * 1024 * 1024
TRANS_B = (((1,), (1,)), ((), ()))


COLUMN_TILES = 4
DEPTH_TILE = 2048
MESH = pl.DeviceIdType.MESH


def flipped(place, mask):
    bits = [(place // b + mask // b) % 2 for b in (1, 2, 4)]
    return bits[0] + 2 * bits[1] + 4 * bits[2]


def greet(peers):
    barrier = pltpu.get_barrier_semaphore()
    for peer in peers:
        pl.semaphore_signal(
            barrier, inc=1, device_id={"frames": peer}, device_id_type=MESH
        )
    pl.semaphore_wait(barrier, len(peers))


def half_norm_of(points):
    wide = points.astype(jnp.float32)
    return 0.5 * jnp.sum(wide * wide, axis=1, keepdims=True)


def weights_of(points, norms, rows):
    score = (
        lax.dot_general(points, rows, TRANS_B, preferred_element_type=jnp.float32) - norms
    )
    top = jnp.max(score, axis=0, keepdims=True)
    return top, jnp.exp2(ALPHA * (score - top))


def members_kernel(
    frames_ref, centers_ref, source_ref,
    member_ref, lead_ref, top_ref, sum_ref, lead_top_ref, halo_top_ref, halo_sum_ref, halo_lead_top_ref,
    rows, tail, halo, own, own_norm, source_norm, member_out, lead_out, halo_out,
    load_sem, out_sem, halo_sem, send_sem, recv_sem,
):
    devices = lax.axis_size("frames")
    me = lax.axis_index("frames")
    plane, place = me // GROUP, me % GROUP
    base = plane * GROUP
    near = {mask: base + flipped(place, mask) for mask in (1, 2, 4)}
    above = lax.rem(me + GROUP, devices)
    below = lax.rem(me + devices - GROUP, devices)
    states = own.shape[0]

    def part(mask, half):
        at = flipped(place, mask)
        return rows.at[pl.ds(pl.multiple_of(at * 2 * TILE + half * TILE, TILE), TILE), :]

    plan = [(mask, half, to) for half in (0, 1) for mask, to in ((0, 1), (0, 2), (0, 4))]
    plan += [(mask, half, 1) for half in (0, 1) for mask in (2, 4)]
    plan += [(4, 0, 2), (2, 1, 4), (6, 0, 1), (6, 1, 1)]
    copies = {}
    for number, (mask, half, to) in enumerate(plan):
        piece = part(mask, half)
        copies[mask, half, to] = pltpu.make_async_remote_copy(
            src_ref=piece, dst_ref=piece,
            send_sem=send_sem.at[number], recv_sem=recv_sem.at[number],
            device_id={"frames": near[to]}, device_id_type=MESH,
        )
    last = rows.shape[0] - TAIL
    tail_copy = pltpu.make_async_remote_copy(
        src_ref=rows.at[pl.ds(last, TAIL), :], dst_ref=tail,
        send_sem=send_sem.at[len(plan)], recv_sem=recv_sem.at[len(plan)],
        device_id={"frames": above}, device_id_type=MESH,
    )

    load_rows = pltpu.make_async_copy(
        frames_ref, rows.at[pl.ds(pl.multiple_of(place * 2 * TILE, TILE), 2 * TILE), :], load_sem.at[0]
    )
    load_own = pltpu.make_async_copy(
        centers_ref.at[pl.ds(pl.multiple_of(place * states, states), states), :], own, load_sem.at[1]
    )
    load_rows.start()
    load_own.start()
    greet([near[1], near[2], near[4], above, below])
    load_rows.wait()
    for half in (0, 1):
        for to in (2, 4, 1):
            copies[0, half, to].start()
    load_own.wait()
    own_norm[...] = half_norm_of(own[...])
    source_norm[...] = half_norm_of(source_ref[...])
    halo[...] = jnp.zeros_like(halo)

    arrivals = {
        2: [((0, 0, 1), [])],
        3: [((0, 1, 1), [])],
        4: [((0, 0, 2), [(2, 0, 1)])],
        5: [((0, 0, 4), [(4, 0, 1), (4, 0, 2)])],
        6: [((2, 0, 1), [])],
        7: [((4, 0, 1), [])],
        8: [((0, 1, 2), [(2, 1, 1), (2, 1, 4)])],
        9: [((0, 1, 4), [(4, 1, 1)])],
        10: [((2, 1, 1), [])],
        11: [((4, 1, 1), [])],
        12: [((4, 0, 2), [(6, 0, 1)])],
        13: [((2, 1, 4), [(6, 1, 1)])],
        14: [((6, 0, 1), [])],
        15: [((6, 1, 1), [])],
    }

    def member_copy(slot, at):
        return pltpu.make_async_copy(
            member_out.at[slot], member_ref.at[:, pl.ds(at, TILE)], out_sem.at[0, slot]
        )

    def lead_copy(slot, at):
        return pltpu.make_async_copy(
            lead_out.at[slot], lead_ref.at[:, pl.ds(at + HALO, TILE)], out_sem.at[1, slot]
        )

    def work(step, carry):
        for number, waits in arrivals.items():
            @pl.when(step == number)
            def _():
                for arrived, onward in waits:
                    copies[arrived].wait_recv()
                    for sent in onward:
                        copies[sent].start()
                if number == 15:
                    tail_copy.start()

        quarter, rest = step // 4, step % 4
        middle = ((quarter + 1) // 2) % 2
        half = middle * (quarter - 1) + (1 - middle) * (rest % 2)
        mask = middle * (2 + 2 * (rest % 2) + rest // 2) + (1 - middle) * (
            6 * (quarter // 3) + rest // 2
        )
        block = 2 * flipped(place, mask) + half
        at = pl.multiple_of(block * TILE, TILE)
        slot = step % 2

        @pl.when(step >= 2)
        def _():
            member_copy(slot, 0).wait()
            lead_copy(slot, 0).wait()

        x = rows[pl.ds(at, TILE), :]
        top, weight = weights_of(own[...], own_norm[...], x)
        top_ref[block] = top
        sum_ref[block] = jnp.sum(weight, axis=0, keepdims=True)
        member_out[slot] = weight.astype(jnp.bfloat16)
        member_copy(slot, at).start()
        top, weight = weights_of(source_ref[...], source_norm[...], x)
        lead_top_ref[block] = top
        lead_out[slot] = weight.astype(jnp.bfloat16)
        lead_copy(slot, at).start()
        return carry

    lax.fori_loop(0, 2 * GROUP, work, 0)

    tail_copy.wait_recv()
    halo[HALO - TAIL :, :] = tail[...]
    x = halo[...]
    top, weight = weights_of(own[...], own_norm[...], x)
    halo_top_ref[...] = top
    halo_sum_ref[...] = jnp.sum(weight, axis=0, keepdims=True)
    top, weight = weights_of(source_ref[...], source_norm[...], x)
    halo_lead_top_ref[...] = top
    halo_out[...] = weight.astype(jnp.bfloat16)
    halo_copy = pltpu.make_async_copy(halo_out, lead_ref.at[:, pl.ds(0, HALO)], halo_sem)
    halo_copy.start()
    for slot in (0, 1):
        member_copy(slot, 0).wait()
        lead_copy(slot, 0).wait()
    halo_copy.wait()
    for copy in copies.values():
        copy.wait_send()
    tail_copy.wait_send()


def members(frames, centers, source):
    frame_count, depth = frames.shape[0] * GROUP, frames.shape[1]
    states = centers.shape[0] // GROUP
    tiles = frame_count // TILE
    stat = jax.ShapeDtypeStruct((tiles, 1, TILE), jnp.float32)
    halo_stat = jax.ShapeDtypeStruct((1, HALO), jnp.float32)
    anywhere = pl.BlockSpec(memory_space=pl.ANY)
    held = pl.BlockSpec(memory_space=pltpu.VMEM)
    return pl.pallas_call(
        members_kernel,
        in_specs=[anywhere, anywhere, held],
        out_specs=[anywhere, anywhere] + [held] * 6,
        out_shape=[
            jax.ShapeDtypeStruct((states, frame_count), jnp.bfloat16),
            jax.ShapeDtypeStruct((W, frame_count + HALO), jnp.bfloat16),
            stat, stat, stat, halo_stat, halo_stat, halo_stat,
        ],
        scratch_shapes=[
            pltpu.VMEM((frame_count, depth), jnp.bfloat16),
            pltpu.VMEM((TAIL, depth), jnp.bfloat16),
            pltpu.VMEM((HALO, depth), jnp.bfloat16),
            pltpu.VMEM((states, depth), jnp.bfloat16),
            pltpu.VMEM((states, 1), jnp.float32),
            pltpu.VMEM((W, 1), jnp.float32),
            pltpu.VMEM((2, states, TILE), jnp.bfloat16),
            pltpu.VMEM((2, W, TILE), jnp.bfloat16),
            pltpu.VMEM((W, HALO), jnp.bfloat16),
            pltpu.SemaphoreType.DMA((2,)),
            pltpu.SemaphoreType.DMA((2, 2)),
            pltpu.SemaphoreType.DMA(()),
            pltpu.SemaphoreType.DMA((16,)),
            pltpu.SemaphoreType.DMA((16,)),
        ],
        compiler_params=pltpu.CompilerParams(
            vmem_limit_bytes=VMEM_BYTES, collective_id=0, has_side_effects=True
        ),
        cost_estimate=pl.CostEstimate(
            flops=2 * frame_count * depth * (states + W),
            bytes_accessed=2 * frame_count * (states + W + depth),
            transcendentals=frame_count * (states + W),
        ),
        name="members",
    )(frames, centers, source)


def counts_kernel(
    planes, factor, lead_ref, scale_ref, member_ref, out_ref,
    lead, slots, total, mine, sent, sent_unit, got, got_unit, summed,
    load_sem, send_sem, recv_sem, unit_send_sem, unit_recv_sem, own_sem, out_send_sem, out_recv_sem,
):
    me = lax.axis_index("frames")
    plane, place = me // GROUP, me % GROUP
    states, frame_count = member_ref.shape
    tile = states // COLUMN_TILES
    plane_rows = W // planes
    owned = plane_rows // GROUP
    planes_away = [lax.rem(plane + d, planes) for d in range(1, planes)]
    others = [plane * GROUP + lax.rem(place + d, GROUP) for d in range(1, GROUP)]

    def load(j, slot):
        return pltpu.make_async_copy(
            member_ref.at[pl.ds(pl.multiple_of(j * tile, tile), tile), :], slots.at[slot], load_sem.at[slot]
        )

    def exchange(j, d):
        to = {"frames": planes_away[d - 1] * GROUP + place}
        return [
            pltpu.make_async_remote_copy(
                src_ref=sent.at[j, d - 1], dst_ref=got.at[j, d - 1],
                send_sem=send_sem.at[j, d - 1], recv_sem=recv_sem.at[j, d - 1],
                device_id=to, device_id_type=MESH,
            ),
            pltpu.make_async_remote_copy(
                src_ref=sent_unit.at[j, d - 1], dst_ref=got_unit.at[j, d - 1],
                send_sem=unit_send_sem.at[j, d - 1], recv_sem=unit_recv_sem.at[j, d - 1],
                device_id=to, device_id_type=MESH,
            ),
        ]

    def columns(j):
        return out_ref.at[:, pl.ds(pl.multiple_of(place * states + j * tile, tile), tile)]

    def hand_out(j, d):
        to = lax.rem(place + d, GROUP)
        return pltpu.make_async_remote_copy(
            src_ref=summed.at[j, pl.ds(pl.multiple_of(to * owned, owned), owned), :], dst_ref=columns(j),
            send_sem=out_send_sem.at[j, d - 1], recv_sem=out_recv_sem.at[j, d - 1],
            device_id={"frames": others[d - 1]}, device_id_type=MESH,
        )

    def keep(j):
        return pltpu.make_async_copy(
            summed.at[j, pl.ds(pl.multiple_of(place * owned, owned), owned), :], columns(j), own_sem.at[j]
        )

    load(0, 0).start()
    greet([away * GROUP + place for away in planes_away] + others)

    def prepare(t, carry):
        at = pl.multiple_of(t * TILE, TILE)
        wide = lead_ref[:, pl.ds(at, TILE + HALO)].astype(jnp.float32)
        moved = pltpu.roll(wide, LAG, 1)[:, HALO:]
        lead[:, pl.ds(at, TILE)] = (moved * scale_ref[:, pl.ds(at, TILE)]).astype(jnp.bfloat16)
        return carry

    lax.fori_loop(0, frame_count // TILE, prepare, 0)

    def work(j, carry):
        slot = j % 2
        load(j, slot).wait()

        @pl.when(j + 1 < COLUMN_TILES)
        def _():
            load(j + 1, (j + 1) % 2).start()

        total[...] = jnp.zeros_like(total)

        def add(t, inner):
            at = pl.ds(pl.multiple_of(t * DEPTH_TILE, DEPTH_TILE), DEPTH_TILE)
            total[...] += lax.dot_general(
                lead[:, at], slots[slot, :, at], TRANS_B, preferred_element_type=jnp.float32
            )
            return inner

        lax.fori_loop(0, frame_count // DEPTH_TILE, add, 0)
        mine[j] = total[pl.ds(pl.multiple_of(plane * plane_rows, plane_rows), plane_rows), :]
        for d in range(1, planes):
            piece = total[
                pl.ds(pl.multiple_of(planes_away[d - 1] * plane_rows, plane_rows), plane_rows), :
            ]
            column_top = jnp.maximum(jnp.max(piece, axis=0, keepdims=True), 1e-30)
            coded = (piece * (32767.0 / column_top) + 0.5).astype(jnp.int32)
            sent[j, d - 1] = jnp.minimum(coded, 32767).astype(jnp.int16)
            sent_unit[j, d - 1] = jnp.broadcast_to(column_top * (factor / 32767.0), (8, tile))
            for copy in exchange(j, d):
                copy.start()
        return carry

    lax.fori_loop(0, COLUMN_TILES, work, 0)

    def finish(j, carry):
        value = mine[j] * factor
        for d in range(1, planes):
            for copy in exchange(j, d):
                copy.wait_recv()
            decoded = got[j, d - 1].astype(jnp.int32).astype(jnp.float32)
            value += decoded * got_unit[j, d - 1][:1, :]
        summed[j] = value
        keep(j).start()
        for d in range(1, GROUP):
            hand_out(j, d).start()
        return carry

    lax.fori_loop(0, COLUMN_TILES, finish, 0)

    def close(j, carry):
        for d in range(1, planes):
            for copy in exchange(j, d):
                copy.wait_send()
        keep(j).wait()
        for d in range(1, GROUP):
            hand_out(j, d).wait_send()
            arrived = lax.rem(place + GROUP - d, GROUP)
            landed = out_ref.at[:, pl.ds(pl.multiple_of(arrived * states + j * tile, tile), tile)]
            pltpu.make_async_remote_copy(
                src_ref=landed, dst_ref=landed,
                send_sem=out_send_sem.at[j, d - 1], recv_sem=out_recv_sem.at[j, d - 1],
                device_id={"frames": others[d - 1]}, device_id_type=MESH,
            ).wait_recv()
        return carry

    lax.fori_loop(0, COLUMN_TILES, close, 0)


def counts_of(lead, scale, member, planes):
    states, frame_count = member.shape
    tile = states // COLUMN_TILES
    plane_rows = W // planes
    owned = plane_rows // GROUP
    held = pl.BlockSpec(memory_space=pltpu.VMEM)
    anywhere = pl.BlockSpec(memory_space=pl.ANY)
    pair = (COLUMN_TILES, planes - 1)
    return pl.pallas_call(
        functools.partial(counts_kernel, planes, K * K / (frame_count * planes)),
        in_specs=[held, held, anywhere],
        out_specs=anywhere,
        out_shape=jax.ShapeDtypeStruct((owned, GROUP * states), jnp.float32),
        scratch_shapes=[
            pltpu.VMEM((W, frame_count), jnp.bfloat16),
            pltpu.VMEM((2, tile, frame_count), jnp.bfloat16),
            pltpu.VMEM((W, tile), jnp.float32),
            pltpu.VMEM((COLUMN_TILES, plane_rows, tile), jnp.float32),
            pltpu.VMEM(pair + (plane_rows, tile), jnp.int16),
            pltpu.VMEM(pair + (8, tile), jnp.float32),
            pltpu.VMEM(pair + (plane_rows, tile), jnp.int16),
            pltpu.VMEM(pair + (8, tile), jnp.float32),
            pltpu.VMEM((COLUMN_TILES, plane_rows, tile), jnp.float32),
            pltpu.SemaphoreType.DMA((2,)),
            pltpu.SemaphoreType.DMA(pair),
            pltpu.SemaphoreType.DMA(pair),
            pltpu.SemaphoreType.DMA(pair),
            pltpu.SemaphoreType.DMA(pair),
            pltpu.SemaphoreType.DMA((COLUMN_TILES,)),
            pltpu.SemaphoreType.DMA((COLUMN_TILES, GROUP - 1)),
            pltpu.SemaphoreType.DMA((COLUMN_TILES, GROUP - 1)),
        ],
        compiler_params=pltpu.CompilerParams(
            vmem_limit_bytes=VMEM_BYTES, collective_id=1, has_side_effects=True
        ),
        cost_estimate=pl.CostEstimate(
            flops=2 * frame_count * W * states,
            bytes_accessed=2 * frame_count * (states + W),
            transcendentals=0,
        ),
        name="counts",
    )(lead, scale, member)


def segment_of(positions, starts):
    return jnp.sum((starts[:, None] <= positions[None, :]).astype(jnp.int32), axis=0)


def shards(frames, centers, starts):
    devices = lax.axis_size("frames")
    planes = devices // GROUP
    plane = lax.axis_index("frames") // GROUP
    groups = [[p * GROUP + c for c in range(GROUP)] for p in range(planes)]

    source = centers[:W]
    if lax.axis_size("centers") > 1:
        mine = lax.axis_index("centers") == 0
        source = lax.psum(jnp.where(mine, source, jnp.zeros_like(source)), "centers")

    member, lead, top, total, lead_top, halo_top, halo_total, halo_lead_top = members(
        frames, centers, source
    )
    plane_frames = member.shape[1]
    top, total, lead_top = (v.reshape(1, plane_frames) for v in (top, total, lead_top))

    stats = jnp.concatenate(
        [
            jnp.concatenate([halo_top, top], axis=1),
            jnp.concatenate([halo_total, total], axis=1),
        ],
        axis=0,
    )
    gathered = lax.all_gather(stats, "frames", axis_index_groups=groups)
    all_top = lax.pmax(jnp.max(gathered[:, 0], axis=0), "centers")
    all_total = lax.psum(
        jnp.sum(gathered[:, 1] * jnp.exp2(ALPHA * (gathered[:, 0] - all_top)), axis=0),
        "centers",
    )

    positions = plane * plane_frames - HALO + jnp.arange(plane_frames + HALO, dtype=jnp.int32)
    usable = jnp.logical_and(
        segment_of(positions, starts) == segment_of(positions + LAG, starts),
        jnp.logical_and(positions >= 0, positions + LAG < plane_frames * planes),
    )
    lead_tops = jnp.concatenate([halo_lead_top, lead_top], axis=1)[0]
    lead_factor = jnp.where(usable, jnp.exp2(ALPHA * (lead_tops - all_top)) / all_total, 0.0)
    lag_factor = jnp.exp2(ALPHA * (top[0] - all_top[HALO:])) / all_total[HALO:]
    scale = lead_factor[HALO - LAG : HALO - LAG + plane_frames] * lag_factor

    return counts_of(lead, scale[None, :], member, planes)


def solution(mesh):
    return jax.shard_map(
        shards,
        mesh=mesh,
        in_specs=(P("frames", None), P("centers", None), P()),
        out_specs=P("frames", "centers"),
        check_vma=False,
    )
```

```python
import functools
import math

import jax
import jax.numpy as jnp
from jax import lax
from jax.experimental import pallas as pl
from jax.experimental.pallas import tpu as pltpu
from jax.sharding import PartitionSpec as P

K = 16384
W = 512
LAG = 5
GROUP = 8
HALO = 128
TAIL = 16
TILE = 512
SHARPNESS = 0.03125
ALPHA = 2.0 * SHARPNESS * math.log2(math.e)
VMEM_BYTES = 56 * 1024 * 1024
TRANS_B = (((1,), (1,)), ((), ()))


COLUMN_TILES = 8
CHUNK = 256
DEPTH_TILE = 2048
MESH = pl.DeviceIdType.MESH


def flipped(place, mask):
    bits = [(place // b + mask // b) % 2 for b in (1, 2, 4)]
    return bits[0] + 2 * bits[1] + 4 * bits[2]


def placed(index):
    return index // 16, (index // 4) % 2, (index // 8) % 2 * 4 + index % 4


def device_at(outer, row, place):
    return outer * 16 + place // 4 * 8 + row * 4 + place % 4


def greet(peers):
    barrier = pltpu.get_barrier_semaphore()
    for peer in peers:
        pl.semaphore_signal(
            barrier, inc=1, device_id={"frames": peer}, device_id_type=MESH
        )
    pl.semaphore_wait(barrier, len(peers))


def folded(values, combine):
    return combine(values.reshape(values.shape[0] // 8, 8, values.shape[1]), axis=0)


def members_kernel(
    frames_ref, centers_ref, source_ref,
    member_ref, lead_ref, top_ref, sum_ref, lead_top_ref, halo_top_ref, halo_sum_ref, halo_lead_top_ref,
    rows, tail, halo, points, norms, score_even, score_odd, member_out, lead_out, halo_out,
    load_sem, out_sem, halo_sem, send_sem, recv_sem, tail_send_sem, tail_recv_sem,
):
    outers = lax.axis_size("frames") // 16
    outer, row, place = placed(lax.axis_index("frames"))
    near = {mask: device_at(outer, row, flipped(place, mask)) for mask in (1, 2, 4)}
    beside = device_at(outer, 1 - row, place)
    across = device_at(lax.rem(outer + 2 * row - 1 + outers, outers), 1 - row, place)
    follows = device_at(lax.rem(outer + row, outers), 1 - row, place)
    states = points.shape[0] - W

    def part(mask, half):
        at = flipped(place, mask)
        return rows.at[pl.ds(pl.multiple_of(at * 2 * TILE + half * TILE, TILE), TILE), :]

    plan = [(mask, half, to) for half in (0, 1) for mask, to in ((0, 1), (0, 2), (0, 4))]
    plan += [(mask, half, 1) for half in (0, 1) for mask in (2, 4)]
    plan += [(4, 0, 2), (2, 1, 4), (6, 0, 1), (6, 1, 1)]
    copies = {}
    for number, (mask, half, to) in enumerate(plan):
        piece = part(mask, half)
        copies[mask, half, to] = pltpu.make_async_remote_copy(
            src_ref=piece, dst_ref=piece,
            send_sem=send_sem.at[number], recv_sem=recv_sem.at[number],
            device_id={"frames": near[to]}, device_id_type=MESH,
        )
    run = rows.shape[0] // 2

    def tail_copy(number, slot, to):
        return pltpu.make_async_remote_copy(
            src_ref=rows.at[pl.ds((number + 1) * run - TAIL, TAIL), :], dst_ref=tail.at[slot],
            send_sem=tail_send_sem.at[number], recv_sem=tail_recv_sem.at[slot],
            device_id={"frames": to}, device_id_type=MESH,
        )

    tails = [tail_copy(0, row, beside), tail_copy(1, 1 - row, follows)]

    load_rows = pltpu.make_async_copy(
        frames_ref, rows.at[pl.ds(pl.multiple_of(place * 2 * TILE, TILE), 2 * TILE), :], load_sem.at[0]
    )
    load_own = pltpu.make_async_copy(
        centers_ref.at[pl.ds(pl.multiple_of(place * states, states), states), :], points.at[pl.ds(0, states), :], load_sem.at[1]
    )
    load_source = pltpu.make_async_copy(source_ref, points.at[pl.ds(states, W), :], load_sem.at[2])
    load_rows.start()
    load_own.start()
    load_source.start()
    greet([near[1], near[2], near[4], beside, across])
    load_rows.wait()
    for half in (0, 1):
        for to in (2, 4, 1):
            copies[0, half, to].start()
    load_own.wait()
    load_source.wait()

    def square(n, carry):
        at = pl.ds(pl.multiple_of(n * CHUNK, CHUNK), CHUNK)
        wide = points[at, :].astype(jnp.float32)
        norm = 0.5 * jnp.sum(wide * wide, axis=1, keepdims=True)
        norms[at, :] = jnp.broadcast_to(norm, (CHUNK, 128))
        return carry

    lax.fori_loop(0, (states + W) // CHUNK, square, 0)
    halo[...] = jnp.zeros_like(halo)

    arrivals = {
        2: [((0, 0, 1), [])],
        3: [((0, 1, 1), [])],
        4: [((0, 0, 2), [(2, 0, 1)])],
        5: [((0, 0, 4), [(4, 0, 1), (4, 0, 2)])],
        6: [((2, 0, 1), [])],
        7: [((4, 0, 1), [])],
        8: [((0, 1, 2), [(2, 1, 1), (2, 1, 4)])],
        9: [((0, 1, 4), [(4, 1, 1)])],
        10: [((2, 1, 1), [])],
        11: [((4, 1, 1), [])],
        12: [((4, 0, 2), [(6, 0, 1)])],
        13: [((2, 1, 4), [(6, 1, 1)])],
        14: [((6, 0, 1), [])],
        15: [((6, 1, 1), [])],
    }

    def member_copy(slot, at):
        return pltpu.make_async_copy(
            member_out.at[slot], member_ref.at[:, pl.ds(at, TILE)], out_sem.at[0, slot]
        )

    def lead_copy(slot, at):
        return pltpu.make_async_copy(
            lead_out.at[slot], lead_ref.at[:, pl.ds(at, TILE)], out_sem.at[1, slot]
        )

    def arrive(step):
        for number, waits in arrivals.items():
            @pl.when(step == number)
            def _():
                for arrived, onward in waits:
                    copies[arrived].wait_recv()
                    for sent in onward:
                        copies[sent].start()
                if number == 15:
                    for copy in tails:
                        copy.start()

    def block_at(step):
        quarter, rest = step // 4, step % 4
        middle = ((quarter + 1) // 2) % 2
        half = middle * (quarter - 1) + (1 - middle) * (rest % 2)
        mask = middle * (2 + 2 * (rest % 2) + rest // 2) + (1 - middle) * (
            6 * (quarter // 3) + rest // 2
        )
        return 2 * flipped(place, mask) + half

    scores = (score_even, score_odd)

    def passes(x, score, done, tops, member_at, lead_at):
        best = [None, None]
        sums = None
        for n in range((states + W) // CHUNK):
            kind = int(n * CHUNK >= states)
            at = slice(n * CHUNK, (n + 1) * CHUNK)
            if x is not None:
                norm = jnp.concatenate([norms[at, :]] * (x.shape[0] // 128), axis=1)
                value = (
                    lax.dot_general(points[at, :], x, TRANS_B, preferred_element_type=jnp.float32)
                    - norm
                )
                score[at, : x.shape[0]] = value
                top = folded(value, jnp.max)
                best[kind] = top if best[kind] is None else jnp.maximum(best[kind], top)
            if done is not None:
                width = tops[kind].shape[1]
                weight = jnp.exp2(ALPHA * (done[at, :width] - tops[kind]))
                if kind == 0:
                    if member_at is not None:
                        member_at[at, :] = weight.astype(jnp.bfloat16)
                    part_sum = folded(weight, jnp.sum)
                    sums = part_sum if sums is None else sums + part_sum
                else:
                    lead_at[n * CHUNK - states : (n + 1) * CHUNK - states, :] = weight.astype(
                        jnp.bfloat16
                    )
        if x is not None:
            best = tuple(jnp.max(b, axis=0, keepdims=True) for b in best)
        if done is not None:
            sums = jnp.sum(sums, axis=0, keepdims=True)
        return best, sums

    def rows_at(block):
        return rows[pl.ds(pl.multiple_of(block * TILE, TILE), TILE), :]

    def turn(step, slot, tops, more=True):
        block = block_at(step)
        x = None
        if more:
            arrive(step + 1)
            x = rows_at(block_at(step + 1))

        @pl.when(step >= 2)
        def _():
            member_copy(slot, 0).wait()
            lead_copy(slot, 0).wait()

        following, sums = passes(
            x, scores[1 - slot], scores[slot], tops, member_out.at[slot], lead_out.at[slot]
        )
        top_ref[block] = tops[0]
        lead_top_ref[block] = tops[1]
        sum_ref[block] = sums
        at = pl.multiple_of(block * TILE, TILE)
        member_copy(slot, at).start()
        lead_copy(slot, pl.multiple_of(at + HALO * (1 + block // GROUP), 128)).start()
        return following

    def work(pair, tops):
        tops = turn(2 * pair, 0, tops)
        return turn(2 * pair + 1, 1, tops)

    tops, _ = passes(rows_at(block_at(jnp.int32(0))), score_even, None, None, None, None)
    tops = lax.fori_loop(0, GROUP - 1, work, tops)
    tops = turn(jnp.int32(2 * GROUP - 2), 0, tops)
    turn(jnp.int32(2 * GROUP - 1), 1, tops, more=False)

    for slot in (0, 1):
        tail_copy(0, slot, beside).wait_recv()
        halo[(slot + 1) * HALO - TAIL : (slot + 1) * HALO, :] = tail[slot]
    tops, _ = passes(halo[...], score_even, None, None, None, None)
    _, sums = passes(None, None, score_even, tops, None, halo_out)
    halo_top_ref[...] = tops[0]
    halo_sum_ref[...] = sums
    halo_lead_top_ref[...] = tops[1]
    halo_copies = [
        pltpu.make_async_copy(
            halo_out.at[:, pl.ds(slot * HALO, HALO)],
            lead_ref.at[:, pl.ds(slot * (HALO + run), HALO)],
            halo_sem.at[slot],
        )
        for slot in (0, 1)
    ]
    for copy in halo_copies:
        copy.start()
    for slot in (0, 1):
        member_copy(slot, 0).wait()
        lead_copy(slot, 0).wait()
    for copy in halo_copies:
        copy.wait()
    for copy in copies.values():
        copy.wait_send()
    for copy in tails:
        copy.wait_send()


def members(frames, centers, source):
    frame_count, depth = frames.shape[0] * GROUP, frames.shape[1]
    states = centers.shape[0] // GROUP
    tiles = frame_count // TILE
    stat = jax.ShapeDtypeStruct((tiles, 1, TILE), jnp.float32)
    halo_stat = jax.ShapeDtypeStruct((1, 2 * HALO), jnp.float32)
    anywhere = pl.BlockSpec(memory_space=pl.ANY)
    held = pl.BlockSpec(memory_space=pltpu.VMEM)
    return pl.pallas_call(
        members_kernel,
        in_specs=[anywhere, anywhere, anywhere],
        out_specs=[anywhere, anywhere] + [held] * 6,
        out_shape=[
            jax.ShapeDtypeStruct((states, frame_count), jnp.bfloat16),
            jax.ShapeDtypeStruct((W, frame_count + 2 * HALO), jnp.bfloat16),
            stat, stat, stat, halo_stat, halo_stat, halo_stat,
        ],
        scratch_shapes=[
            pltpu.VMEM((frame_count, depth), jnp.bfloat16),
            pltpu.VMEM((2, TAIL, depth), jnp.bfloat16),
            pltpu.VMEM((2 * HALO, depth), jnp.bfloat16),
            pltpu.VMEM((states + W, depth), jnp.bfloat16),
            pltpu.VMEM((states + W, 128), jnp.float32),
            pltpu.VMEM((states + W, TILE), jnp.float32),
            pltpu.VMEM((states + W, TILE), jnp.float32),
            pltpu.VMEM((2, states, TILE), jnp.bfloat16),
            pltpu.VMEM((2, W, TILE), jnp.bfloat16),
            pltpu.VMEM((W, 2 * HALO), jnp.bfloat16),
            pltpu.SemaphoreType.DMA((3,)),
            pltpu.SemaphoreType.DMA((2, 2)),
            pltpu.SemaphoreType.DMA((2,)),
            pltpu.SemaphoreType.DMA((16,)),
            pltpu.SemaphoreType.DMA((16,)),
            pltpu.SemaphoreType.DMA((2,)),
            pltpu.SemaphoreType.DMA((2,)),
        ],
        compiler_params=pltpu.CompilerParams(
            vmem_limit_bytes=VMEM_BYTES, collective_id=0, has_side_effects=True
        ),
        cost_estimate=pl.CostEstimate(
            flops=2 * frame_count * depth * (states + W),
            bytes_accessed=2 * frame_count * (states + W + depth),
            transcendentals=frame_count * (states + W),
        ),
        name="members",
    )(frames, centers, source)


def coded(piece, factor):
    column_top = jnp.maximum(jnp.max(piece, axis=0, keepdims=True), 1e-30)
    steps = (piece * (32767.0 / column_top) + 0.5).astype(jnp.int32)
    unit = jnp.broadcast_to(column_top * (factor / 32767.0), (8, piece.shape[1]))
    return jnp.minimum(steps, 32767).astype(jnp.int16), unit


def decoded(steps, unit):
    return steps.astype(jnp.int32).astype(jnp.float32) * unit[:1, :]


def counts_kernel(
    outers, factor, lead_ref, scale_ref, member_ref, out_ref,
    lead, slots, total, half, half_sent, half_unit, half_got, half_got_unit,
    mine, sent, sent_unit, got, got_unit, summed,
    load_sem, half_sem, send_sem, recv_sem, unit_send_sem, unit_recv_sem, own_sem, out_send_sem, out_recv_sem,
):
    outer, row, place = placed(lax.axis_index("frames"))
    states, frame_count = member_ref.shape
    tile = max(128, states // COLUMN_TILES)
    tiles = states // tile
    outer_rows = W // 2 // outers
    owned = outer_rows // GROUP
    beside = device_at(outer, 1 - row, place)
    outers_away = [lax.rem(outer + d, outers) for d in range(1, outers)]
    others = [device_at(outer, row, lax.rem(place + d, GROUP)) for d in range(1, GROUP)]

    def load(j, slot):
        return pltpu.make_async_copy(
            member_ref.at[pl.ds(pl.multiple_of(j * tile, tile), tile), :], slots.at[slot], load_sem.at[slot]
        )

    def remote(source, target, send, recv, to):
        return pltpu.make_async_remote_copy(
            src_ref=source, dst_ref=target, send_sem=send, recv_sem=recv,
            device_id={"frames": to}, device_id_type=MESH,
        )

    def halves(j):
        return [
            remote(half_sent.at[j], half_got.at[j], half_sem.at[0, j], half_sem.at[1, j], beside),
            remote(half_unit.at[j], half_got_unit.at[j], half_sem.at[2, j], half_sem.at[3, j], beside),
        ]

    def exchange(j, d):
        to = device_at(outers_away[d - 1], row, place)
        at = (j, d - 1)
        return [
            remote(sent.at[at], got.at[at], send_sem.at[at], recv_sem.at[at], to),
            remote(sent_unit.at[at], got_unit.at[at], unit_send_sem.at[at], unit_recv_sem.at[at], to),
        ]

    def columns(j, whose):
        return out_ref.at[:, pl.ds(pl.multiple_of(whose * states + j * tile, tile), tile)]

    def hand_out(j, d):
        to = lax.rem(place + d, GROUP)
        return remote(
            summed.at[j, pl.ds(pl.multiple_of(to * owned, owned), owned), :], columns(j, place),
            out_send_sem.at[j, d - 1], out_recv_sem.at[j, d - 1], others[d - 1],
        )

    def keep(j):
        return pltpu.make_async_copy(
            summed.at[j, pl.ds(pl.multiple_of(place * owned, owned), owned), :], columns(j, place), own_sem.at[j]
        )

    load(0, 0).start()
    greet([beside] + [device_at(away, row, place) for away in outers_away] + others)

    def prepare(t, carry):
        at = pl.multiple_of(t * TILE, TILE)
        before = pl.multiple_of(at + HALO * (t // GROUP), 128)
        wide = lead_ref[:, pl.ds(before, TILE + HALO)].astype(jnp.float32)
        moved = pltpu.roll(wide, LAG, 1)[:, HALO:]
        lead[:, pl.ds(at, TILE)] = (moved * scale_ref[:, pl.ds(at, TILE)]).astype(jnp.bfloat16)
        return carry

    lax.fori_loop(0, frame_count // TILE, prepare, 0)

    def compute(j):
        slot = j % 2
        load(j, slot).wait()

        @pl.when(j + 1 < tiles)
        def _():
            load(j + 1, (j + 1) % 2).start()

        total[...] = jnp.zeros_like(total)

        def add(t, inner):
            at = pl.ds(pl.multiple_of(t * DEPTH_TILE, DEPTH_TILE), DEPTH_TILE)
            total[...] += lax.dot_general(
                lead[:, at], slots[slot, :, at], TRANS_B, preferred_element_type=jnp.float32
            )
            return inner

        lax.fori_loop(0, frame_count // DEPTH_TILE, add, 0)
        half_sent[j], half_unit[j] = coded(
            total[pl.ds(pl.multiple_of((1 - row) * (W // 2), W // 2), W // 2), :], 1.0
        )
        for copy in halves(j):
            copy.start()
        half[j] = total[pl.ds(pl.multiple_of(row * (W // 2), W // 2), W // 2), :]

    def merge(j):
        for copy in halves(j):
            copy.wait_recv()
        half[j] += decoded(half_got[j], half_got_unit[j])
        for d in range(1, outers):
            at = pl.multiple_of(outers_away[d - 1] * outer_rows, outer_rows)
            sent[j, d - 1], sent_unit[j, d - 1] = coded(half[j, pl.ds(at, outer_rows), :], factor)
            for copy in exchange(j, d):
                copy.start()
        mine[j] = half[j, pl.ds(pl.multiple_of(outer * outer_rows, outer_rows), outer_rows), :]

    def finish(j):
        value = mine[j] * factor
        for d in range(1, outers):
            for copy in exchange(j, d):
                copy.wait_recv()
            value += decoded(got[j, d - 1], got_unit[j, d - 1])
        summed[j] = value
        keep(j).start()
        for d in range(1, GROUP):
            hand_out(j, d).start()

    def work(step, carry):
        pl.when(step < tiles)(lambda: compute(step))
        pl.when(jnp.logical_and(step >= 2, step < tiles + 2))(lambda: merge(step - 2))
        pl.when(step >= 5)(lambda: finish(step - 5))
        return carry

    lax.fori_loop(0, tiles + 5, work, 0)

    def close(j, carry):
        for copy in halves(j):
            copy.wait_send()
        for d in range(1, outers):
            for copy in exchange(j, d):
                copy.wait_send()
        keep(j).wait()
        for d in range(1, GROUP):
            hand_out(j, d).wait_send()
            landed = columns(j, lax.rem(place + GROUP - d, GROUP))
            remote(
                landed, landed, out_send_sem.at[j, d - 1], out_recv_sem.at[j, d - 1], others[d - 1]
            ).wait_recv()
        return carry

    lax.fori_loop(0, tiles, close, 0)


def counts_of(lead, scale, member, outers):
    states, frame_count = member.shape
    tile = max(128, states // COLUMN_TILES)
    tiles = states // tile
    outer_rows = W // 2 // outers
    owned = outer_rows // GROUP
    held = pl.BlockSpec(memory_space=pltpu.VMEM)
    anywhere = pl.BlockSpec(memory_space=pl.ANY)
    pair = (tiles, outers - 1)
    return pl.pallas_call(
        functools.partial(counts_kernel, outers, K * K / (2 * frame_count * outers)),
        in_specs=[held, held, anywhere],
        out_specs=anywhere,
        out_shape=jax.ShapeDtypeStruct((owned, GROUP * states), jnp.float32),
        scratch_shapes=[
            pltpu.VMEM((W, frame_count), jnp.bfloat16),
            pltpu.VMEM((2, tile, frame_count), jnp.bfloat16),
            pltpu.VMEM((W, tile), jnp.float32),
            pltpu.VMEM((tiles, W // 2, tile), jnp.float32),
            pltpu.VMEM((tiles, W // 2, tile), jnp.int16),
            pltpu.VMEM((tiles, 8, tile), jnp.float32),
            pltpu.VMEM((tiles, W // 2, tile), jnp.int16),
            pltpu.VMEM((tiles, 8, tile), jnp.float32),
            pltpu.VMEM((tiles, outer_rows, tile), jnp.float32),
            pltpu.VMEM(pair + (outer_rows, tile), jnp.int16),
            pltpu.VMEM(pair + (8, tile), jnp.float32),
            pltpu.VMEM(pair + (outer_rows, tile), jnp.int16),
            pltpu.VMEM(pair + (8, tile), jnp.float32),
            pltpu.VMEM((tiles, outer_rows, tile), jnp.float32),
            pltpu.SemaphoreType.DMA((2,)),
            pltpu.SemaphoreType.DMA((4, tiles)),
            pltpu.SemaphoreType.DMA(pair),
            pltpu.SemaphoreType.DMA(pair),
            pltpu.SemaphoreType.DMA(pair),
            pltpu.SemaphoreType.DMA(pair),
            pltpu.SemaphoreType.DMA((tiles,)),
            pltpu.SemaphoreType.DMA((tiles, GROUP - 1)),
            pltpu.SemaphoreType.DMA((tiles, GROUP - 1)),
        ],
        compiler_params=pltpu.CompilerParams(
            vmem_limit_bytes=VMEM_BYTES, collective_id=1, has_side_effects=True
        ),
        cost_estimate=pl.CostEstimate(
            flops=2 * frame_count * W * states,
            bytes_accessed=2 * frame_count * (states + W),
            transcendentals=0,
        ),
        name="counts",
    )(lead, scale, member)


def segment_of(positions, starts):
    return jnp.sum((starts[:, None] <= positions[None, :]).astype(jnp.int32), axis=0)


def shards(frames, centers, starts):
    devices = lax.axis_size("frames")
    outers = devices // 16
    outer, row, _ = placed(lax.axis_index("frames"))
    groups = [[device_at(o, r, p) for p in range(GROUP)] for o in range(outers) for r in (0, 1)]

    source = centers[:W]
    if lax.axis_size("centers") > 1:
        mine = lax.axis_index("centers") == 0
        source = lax.psum(jnp.where(mine, source, jnp.zeros_like(source)), "centers")
    source = source.reshape(outers, 2, 2, -1, source.shape[1]).transpose(2, 0, 1, 3, 4)
    source = source.reshape(W, -1)

    member, lead, top, total, lead_top, halo_top, halo_total, halo_lead_top = members(
        frames, centers, source
    )
    group_frames = member.shape[1]
    run = group_frames // 2

    def with_halos(values, halos):
        return jnp.concatenate(
            [halos.reshape(2, HALO), values.reshape(2, run)], axis=1
        ).reshape(1, -1)

    def without_halos(values):
        return values.reshape(2, HALO + run)[:, HALO:].reshape(group_frames)

    stats = jnp.concatenate([with_halos(top, halo_top), with_halos(total, halo_total)], axis=0)
    gathered = lax.all_gather(stats, "frames", axis_index_groups=groups)
    all_top = lax.pmax(jnp.max(gathered[:, 0], axis=0), "centers")
    all_total = lax.psum(
        jnp.sum(gathered[:, 1] * jnp.exp2(ALPHA * (gathered[:, 0] - all_top)), axis=0),
        "centers",
    )

    device_frames = frames.shape[0]
    first = jnp.stack([device_at(outer, row, 0), device_at(outer, row, 4)]) * device_frames
    positions = first[:, None] + jnp.arange(-HALO, run, dtype=jnp.int32)[None, :]
    positions = positions.reshape(-1)
    usable = jnp.logical_and(
        segment_of(positions, starts) == segment_of(positions + LAG, starts),
        jnp.logical_and(positions >= 0, positions + LAG < device_frames * devices),
    )
    lead_tops = with_halos(lead_top, halo_lead_top)[0]
    lead_factor = jnp.where(usable, jnp.exp2(ALPHA * (lead_tops - all_top)) / all_total, 0.0)
    lag_factor = jnp.exp2(ALPHA * (with_halos(top, halo_top)[0] - all_top)) / all_total
    moved = lead_factor.reshape(2, HALO + run)[:, HALO - LAG : HALO - LAG + run]
    scale = moved.reshape(group_frames) * without_halos(lag_factor)
    return counts_of(lead, scale[None, :], member, outers)


def solution(mesh):
    return jax.shard_map(
        shards,
        mesh=mesh,
        in_specs=(P("frames", None), P("centers", None), P()),
        out_specs=P("frames", "centers"),
        check_vma=False,
    )
```

```python
import functools
import math

import jax
import jax.numpy as jnp
from jax import lax
from jax.experimental import pallas as pl
from jax.experimental.pallas import tpu as pltpu
from jax.sharding import PartitionSpec as P

K = 16384
W = 512
LAG = 5
GROUP = 8
HALO = 128
TAIL = 16
TILE = 512
SHARPNESS = 0.03125
ALPHA = 2.0 * SHARPNESS * math.log2(math.e)
VMEM_BYTES = 56 * 1024 * 1024
TRANS_B = (((1,), (1,)), ((), ()))


COLUMN_TILES = 8
CHUNK = 256
DEPTH_TILE = 2048
MESH = pl.DeviceIdType.MESH


def flipped(place, mask):
    bits = [(place // b + mask // b) % 2 for b in (1, 2, 4)]
    return bits[0] + 2 * bits[1] + 4 * bits[2]


def placed(index):
    return index // 16, (index // 4) % 2, (index // 8) % 2 * 4 + index % 4


def device_at(outer, row, place):
    return outer * 16 + place // 4 * 8 + row * 4 + place % 4


def greet(peers):
    barrier = pltpu.get_barrier_semaphore()
    for peer in peers:
        pl.semaphore_signal(
            barrier, inc=1, device_id={"frames": peer}, device_id_type=MESH
        )
    pl.semaphore_wait(barrier, len(peers))


def folded(values, combine):
    return combine(values.reshape(values.shape[0] // 8, 8, values.shape[1]), axis=0)


def members_kernel(
    frames_ref, centers_ref, source_ref,
    member_ref, lead_ref, top_ref, sum_ref, lead_top_ref, halo_top_ref, halo_sum_ref, halo_lead_top_ref,
    rows, tail, halo, points, norms, score_even, score_odd, member_out, lead_out, halo_out,
    load_sem, out_sem, halo_sem, send_sem, recv_sem, tail_send_sem, tail_recv_sem,
):
    outers = lax.axis_size("frames") // 16
    outer, row, place = placed(lax.axis_index("frames"))
    near = {mask: device_at(outer, row, flipped(place, mask)) for mask in (1, 2, 4)}
    beside = device_at(outer, 1 - row, place)
    across = device_at(lax.rem(outer + 2 * row - 1 + outers, outers), 1 - row, place)
    follows = device_at(lax.rem(outer + row, outers), 1 - row, place)
    states = points.shape[0] - W

    def part(mask, half):
        at = flipped(place, mask)
        return rows.at[pl.ds(pl.multiple_of(at * 2 * TILE + half * TILE, TILE), TILE), :]

    plan = [(mask, half, to) for half in (0, 1) for mask, to in ((0, 1), (0, 2), (0, 4))]
    plan += [(mask, half, 1) for half in (0, 1) for mask in (2, 4)]
    plan += [(4, 0, 2), (2, 1, 4), (6, 0, 1), (6, 1, 1)]
    copies = {}
    for number, (mask, half, to) in enumerate(plan):
        piece = part(mask, half)
        copies[mask, half, to] = pltpu.make_async_remote_copy(
            src_ref=piece, dst_ref=piece,
            send_sem=send_sem.at[number], recv_sem=recv_sem.at[number],
            device_id={"frames": near[to]}, device_id_type=MESH,
        )
    run = rows.shape[0] // 2

    def tail_copy(number, slot, to):
        return pltpu.make_async_remote_copy(
            src_ref=rows.at[pl.ds((number + 1) * run - TAIL, TAIL), :], dst_ref=tail.at[slot],
            send_sem=tail_send_sem.at[number], recv_sem=tail_recv_sem.at[slot],
            device_id={"frames": to}, device_id_type=MESH,
        )

    tails = [tail_copy(0, row, beside), tail_copy(1, 1 - row, follows)]

    load_rows = pltpu.make_async_copy(
        frames_ref, rows.at[pl.ds(pl.multiple_of(place * 2 * TILE, TILE), 2 * TILE), :], load_sem.at[0]
    )
    load_own = pltpu.make_async_copy(
        centers_ref.at[pl.ds(pl.multiple_of(place * states, states), states), :], points.at[pl.ds(0, states), :], load_sem.at[1]
    )
    load_source = pltpu.make_async_copy(source_ref, points.at[pl.ds(states, W), :], load_sem.at[2])
    load_rows.start()
    load_own.start()
    load_source.start()
    greet([near[1], near[2], near[4], beside, across])
    load_rows.wait()
    for half in (0, 1):
        for to in (2, 4, 1):
            copies[0, half, to].start()
    load_own.wait()
    load_source.wait()

    def square(n, carry):
        at = pl.ds(pl.multiple_of(n * CHUNK, CHUNK), CHUNK)
        wide = points[at, :].astype(jnp.float32)
        norm = 0.5 * jnp.sum(wide * wide, axis=1, keepdims=True)
        norms[at, :] = jnp.broadcast_to(norm, (CHUNK, 128))
        return carry

    lax.fori_loop(0, (states + W) // CHUNK, square, 0)
    halo[...] = jnp.zeros_like(halo)

    arrivals = {
        2: [((0, 0, 1), [])],
        3: [((0, 1, 1), [])],
        4: [((0, 0, 2), [(2, 0, 1)])],
        5: [((0, 0, 4), [(4, 0, 1), (4, 0, 2)])],
        6: [((2, 0, 1), [])],
        7: [((4, 0, 1), [])],
        8: [((0, 1, 2), [(2, 1, 1), (2, 1, 4)])],
        9: [((0, 1, 4), [(4, 1, 1)])],
        10: [((2, 1, 1), [])],
        11: [((4, 1, 1), [])],
        12: [((4, 0, 2), [(6, 0, 1)])],
        13: [((2, 1, 4), [(6, 1, 1)])],
        14: [((6, 0, 1), [])],
        15: [((6, 1, 1), [])],
    }

    def member_copy(slot, at):
        return pltpu.make_async_copy(
            member_out.at[slot], member_ref.at[:, pl.ds(at, TILE)], out_sem.at[0, slot]
        )

    def lead_copy(slot, at):
        return pltpu.make_async_copy(
            lead_out.at[slot], lead_ref.at[:, pl.ds(at, TILE)], out_sem.at[1, slot]
        )

    def arrive(step):
        for number, waits in arrivals.items():
            @pl.when(step == number)
            def _():
                for arrived, onward in waits:
                    copies[arrived].wait_recv()
                    for sent in onward:
                        copies[sent].start()
                if number == 15:
                    for copy in tails:
                        copy.start()

    def block_at(step):
        quarter, rest = step // 4, step % 4
        middle = ((quarter + 1) // 2) % 2
        half = middle * (quarter - 1) + (1 - middle) * (rest % 2)
        mask = middle * (2 + 2 * (rest % 2) + rest // 2) + (1 - middle) * (
            6 * (quarter // 3) + rest // 2
        )
        return 2 * flipped(place, mask) + half

    scores = (score_even, score_odd)

    def passes(x, score, done, tops, member_at, lead_at):
        best = [None, None]
        sums = None
        for n in range((states + W) // CHUNK):
            kind = int(n * CHUNK >= states)
            at = slice(n * CHUNK, (n + 1) * CHUNK)
            if x is not None:
                norm = jnp.concatenate([norms[at, :]] * (x.shape[0] // 128), axis=1)
                value = (
                    lax.dot_general(points[at, :], x, TRANS_B, preferred_element_type=jnp.float32)
                    - norm
                )
                score[at, : x.shape[0]] = value
                top = folded(value, jnp.max)
                best[kind] = top if best[kind] is None else jnp.maximum(best[kind], top)
            if done is not None:
                width = tops[kind].shape[1]
                weight = jnp.exp2(ALPHA * (done[at, :width] - tops[kind]))
                if kind == 0:
                    if member_at is not None:
                        member_at[at, :] = weight.astype(jnp.bfloat16)
                    part_sum = folded(weight, jnp.sum)
                    sums = part_sum if sums is None else sums + part_sum
                else:
                    lead_at[n * CHUNK - states : (n + 1) * CHUNK - states, :] = weight.astype(
                        jnp.bfloat16
                    )
        if x is not None:
            best = tuple(jnp.max(b, axis=0, keepdims=True) for b in best)
        if done is not None:
            sums = jnp.sum(sums, axis=0, keepdims=True)
        return best, sums

    def rows_at(block):
        return rows[pl.ds(pl.multiple_of(block * TILE, TILE), TILE), :]

    def turn(step, slot, tops, more=True):
        block = block_at(step)
        x = None
        if more:
            arrive(step + 1)
            x = rows_at(block_at(step + 1))

        @pl.when(step >= 2)
        def _():
            member_copy(slot, 0).wait()
            lead_copy(slot, 0).wait()

        following, sums = passes(
            x, scores[1 - slot], scores[slot], tops, member_out.at[slot], lead_out.at[slot]
        )
        top_ref[block] = tops[0]
        lead_top_ref[block] = tops[1]
        sum_ref[block] = sums
        at = pl.multiple_of(block * TILE, TILE)
        member_copy(slot, at).start()
        lead_copy(slot, pl.multiple_of(at + HALO * (1 + block // GROUP), 128)).start()
        return following

    def work(pair, tops):
        tops = turn(2 * pair, 0, tops)
        return turn(2 * pair + 1, 1, tops)

    tops, _ = passes(rows_at(block_at(jnp.int32(0))), score_even, None, None, None, None)
    tops = lax.fori_loop(0, GROUP - 1, work, tops)
    tops = turn(jnp.int32(2 * GROUP - 2), 0, tops)
    turn(jnp.int32(2 * GROUP - 1), 1, tops, more=False)

    for slot in (0, 1):
        tail_copy(0, slot, beside).wait_recv()
        halo[(slot + 1) * HALO - TAIL : (slot + 1) * HALO, :] = tail[slot]
    tops, _ = passes(halo[...], score_even, None, None, None, None)
    _, sums = passes(None, None, score_even, tops, None, halo_out)
    halo_top_ref[...] = tops[0]
    halo_sum_ref[...] = sums
    halo_lead_top_ref[...] = tops[1]
    halo_copies = [
        pltpu.make_async_copy(
            halo_out.at[:, pl.ds(slot * HALO, HALO)],
            lead_ref.at[:, pl.ds(slot * (HALO + run), HALO)],
            halo_sem.at[slot],
        )
        for slot in (0, 1)
    ]
    for copy in halo_copies:
        copy.start()
    for slot in (0, 1):
        member_copy(slot, 0).wait()
        lead_copy(slot, 0).wait()
    for copy in halo_copies:
        copy.wait()
    for copy in copies.values():
        copy.wait_send()
    for copy in tails:
        copy.wait_send()


def members(frames, centers, source):
    frame_count, depth = frames.shape[0] * GROUP, frames.shape[1]
    states = centers.shape[0] // GROUP
    tiles = frame_count // TILE
    stat = jax.ShapeDtypeStruct((tiles, 1, TILE), jnp.float32)
    halo_stat = jax.ShapeDtypeStruct((1, 2 * HALO), jnp.float32)
    anywhere = pl.BlockSpec(memory_space=pl.ANY)
    held = pl.BlockSpec(memory_space=pltpu.VMEM)
    return pl.pallas_call(
        members_kernel,
        in_specs=[anywhere, anywhere, anywhere],
        out_specs=[anywhere, anywhere] + [held] * 6,
        out_shape=[
            jax.ShapeDtypeStruct((states, frame_count), jnp.bfloat16),
            jax.ShapeDtypeStruct((W, frame_count + 2 * HALO), jnp.bfloat16),
            stat, stat, stat, halo_stat, halo_stat, halo_stat,
        ],
        scratch_shapes=[
            pltpu.VMEM((frame_count, depth), jnp.bfloat16),
            pltpu.VMEM((2, TAIL, depth), jnp.bfloat16),
            pltpu.VMEM((2 * HALO, depth), jnp.bfloat16),
            pltpu.VMEM((states + W, depth), jnp.bfloat16),
            pltpu.VMEM((states + W, 128), jnp.float32),
            pltpu.VMEM((states + W, TILE), jnp.float32),
            pltpu.VMEM((states + W, TILE), jnp.float32),
            pltpu.VMEM((2, states, TILE), jnp.bfloat16),
            pltpu.VMEM((2, W, TILE), jnp.bfloat16),
            pltpu.VMEM((W, 2 * HALO), jnp.bfloat16),
            pltpu.SemaphoreType.DMA((3,)),
            pltpu.SemaphoreType.DMA((2, 2)),
            pltpu.SemaphoreType.DMA((2,)),
            pltpu.SemaphoreType.DMA((16,)),
            pltpu.SemaphoreType.DMA((16,)),
            pltpu.SemaphoreType.DMA((2,)),
            pltpu.SemaphoreType.DMA((2,)),
        ],
        compiler_params=pltpu.CompilerParams(
            vmem_limit_bytes=VMEM_BYTES, collective_id=0, has_side_effects=True
        ),
        cost_estimate=pl.CostEstimate(
            flops=2 * frame_count * depth * (states + W),
            bytes_accessed=2 * frame_count * (states + W + depth),
            transcendentals=frame_count * (states + W),
        ),
        name="members",
    )(frames, centers, source)


def coded(piece, factor):
    column_top = jnp.maximum(jnp.max(piece, axis=0, keepdims=True), 1e-30)
    steps = (piece * (32767.0 / column_top) + 0.5).astype(jnp.int32)
    unit = jnp.broadcast_to(column_top * (factor / 32767.0), (8, piece.shape[1]))
    return jnp.minimum(steps, 32767).astype(jnp.int16), unit


def decoded(steps, unit):
    return steps.astype(jnp.int32).astype(jnp.float32) * unit[:1, :]


def counts_kernel(
    outers, factor, lead_ref, scale_ref, member_ref, out_ref,
    lead, slots, total, half, half_sent, half_unit, half_got, half_got_unit,
    mine, sent, sent_unit, got, got_unit, summed,
    load_sem, half_sem, send_sem, recv_sem, unit_send_sem, unit_recv_sem, own_sem, out_send_sem, out_recv_sem,
):
    outer, row, place = placed(lax.axis_index("frames"))
    states, frame_count = member_ref.shape
    tile = max(128, states // COLUMN_TILES)
    tiles = states // tile
    outer_rows = W // 2 // outers
    owned = outer_rows // GROUP
    beside = device_at(outer, 1 - row, place)
    outers_away = [lax.rem(outer + d, outers) for d in range(1, outers)]
    others = [device_at(outer, row, lax.rem(place + d, GROUP)) for d in range(1, GROUP)]

    def load(j, slot):
        return pltpu.make_async_copy(
            member_ref.at[pl.ds(pl.multiple_of(j * tile, tile), tile), :], slots.at[slot], load_sem.at[slot]
        )

    def remote(source, target, send, recv, to):
        return pltpu.make_async_remote_copy(
            src_ref=source, dst_ref=target, send_sem=send, recv_sem=recv,
            device_id={"frames": to}, device_id_type=MESH,
        )

    def halves(j):
        return [
            remote(half_sent.at[j], half_got.at[j], half_sem.at[0, j], half_sem.at[1, j], beside),
            remote(half_unit.at[j], half_got_unit.at[j], half_sem.at[2, j], half_sem.at[3, j], beside),
        ]

    def exchange(j, d):
        to = device_at(outers_away[d - 1], row, place)
        at = (j, d - 1)
        return [
            remote(sent.at[at], got.at[at], send_sem.at[at], recv_sem.at[at], to),
            remote(sent_unit.at[at], got_unit.at[at], unit_send_sem.at[at], unit_recv_sem.at[at], to),
        ]

    def columns(j, whose):
        return out_ref.at[:, pl.ds(pl.multiple_of(whose * states + j * tile, tile), tile)]

    def hand_out(j, d):
        to = lax.rem(place + d, GROUP)
        return remote(
            summed.at[j, pl.ds(pl.multiple_of(to * owned, owned), owned), :], columns(j, place),
            out_send_sem.at[j, d - 1], out_recv_sem.at[j, d - 1], others[d - 1],
        )

    def keep(j):
        return pltpu.make_async_copy(
            summed.at[j, pl.ds(pl.multiple_of(place * owned, owned), owned), :], columns(j, place), own_sem.at[j]
        )

    load(0, 0).start()
    greet([beside] + [device_at(away, row, place) for away in outers_away] + others)

    def prepare(t, carry):
        at = pl.multiple_of(t * TILE, TILE)
        before = pl.multiple_of(at + HALO * (t // GROUP), 128)
        wide = lead_ref[:, pl.ds(before, TILE + HALO)].astype(jnp.float32)
        moved = pltpu.roll(wide, LAG, 1)[:, HALO:]
        lead[:, pl.ds(at, TILE)] = (moved * scale_ref[:, pl.ds(at, TILE)]).astype(jnp.bfloat16)
        return carry

    lax.fori_loop(0, frame_count // TILE, prepare, 0)

    def compute(j):
        slot = j % 2
        load(j, slot).wait()

        @pl.when(j + 1 < tiles)
        def _():
            load(j + 1, (j + 1) % 2).start()

        total[...] = jnp.zeros_like(total)

        def add(t, inner):
            at = pl.ds(pl.multiple_of(t * DEPTH_TILE, DEPTH_TILE), DEPTH_TILE)
            total[...] += lax.dot_general(
                lead[:, at], slots[slot, :, at], TRANS_B, preferred_element_type=jnp.float32
            )
            return inner

        lax.fori_loop(0, frame_count // DEPTH_TILE, add, 0)
        half_sent[j], half_unit[j] = coded(
            total[pl.ds(pl.multiple_of((1 - row) * (W // 2), W // 2), W // 2), :], 1.0
        )
        for copy in halves(j):
            copy.start()
        half[j] = total[pl.ds(pl.multiple_of(row * (W // 2), W // 2), W // 2), :]

    def merge(j):
        for copy in halves(j):
            copy.wait_recv()
        half[j] += decoded(half_got[j], half_got_unit[j])
        for d in range(1, outers):
            at = pl.multiple_of(outers_away[d - 1] * outer_rows, outer_rows)
            sent[j, d - 1], sent_unit[j, d - 1] = coded(half[j, pl.ds(at, outer_rows), :], factor)
            for copy in exchange(j, d):
                copy.start()
        mine[j] = half[j, pl.ds(pl.multiple_of(outer * outer_rows, outer_rows), outer_rows), :]

    def finish(j):
        value = mine[j] * factor
        for d in range(1, outers):
            for copy in exchange(j, d):
                copy.wait_recv()
            value += decoded(got[j, d - 1], got_unit[j, d - 1])
        summed[j] = value
        keep(j).start()
        for d in range(1, GROUP):
            hand_out(j, d).start()

    def work(step, carry):
        pl.when(step < tiles)(lambda: compute(step))
        pl.when(jnp.logical_and(step >= 1, step < tiles + 1))(lambda: merge(step - 1))
        pl.when(step >= 4)(lambda: finish(step - 4))
        return carry

    lax.fori_loop(0, tiles + 4, work, 0)

    def close(j, carry):
        for copy in halves(j):
            copy.wait_send()
        for d in range(1, outers):
            for copy in exchange(j, d):
                copy.wait_send()
        keep(j).wait()
        for d in range(1, GROUP):
            hand_out(j, d).wait_send()
            landed = columns(j, lax.rem(place + GROUP - d, GROUP))
            remote(
                landed, landed, out_send_sem.at[j, d - 1], out_recv_sem.at[j, d - 1], others[d - 1]
            ).wait_recv()
        return carry

    lax.fori_loop(0, tiles, close, 0)


def counts_of(lead, scale, member, outers):
    states, frame_count = member.shape
    tile = max(128, states // COLUMN_TILES)
    tiles = states // tile
    outer_rows = W // 2 // outers
    owned = outer_rows // GROUP
    held = pl.BlockSpec(memory_space=pltpu.VMEM)
    anywhere = pl.BlockSpec(memory_space=pl.ANY)
    pair = (tiles, outers - 1)
    return pl.pallas_call(
        functools.partial(counts_kernel, outers, K * K / (2 * frame_count * outers)),
        in_specs=[held, held, anywhere],
        out_specs=anywhere,
        out_shape=jax.ShapeDtypeStruct((owned, GROUP * states), jnp.float32),
        scratch_shapes=[
            pltpu.VMEM((W, frame_count), jnp.bfloat16),
            pltpu.VMEM((2, tile, frame_count), jnp.bfloat16),
            pltpu.VMEM((W, tile), jnp.float32),
            pltpu.VMEM((tiles, W // 2, tile), jnp.float32),
            pltpu.VMEM((tiles, W // 2, tile), jnp.int16),
            pltpu.VMEM((tiles, 8, tile), jnp.float32),
            pltpu.VMEM((tiles, W // 2, tile), jnp.int16),
            pltpu.VMEM((tiles, 8, tile), jnp.float32),
            pltpu.VMEM((tiles, outer_rows, tile), jnp.float32),
            pltpu.VMEM(pair + (outer_rows, tile), jnp.int16),
            pltpu.VMEM(pair + (8, tile), jnp.float32),
            pltpu.VMEM(pair + (outer_rows, tile), jnp.int16),
            pltpu.VMEM(pair + (8, tile), jnp.float32),
            pltpu.VMEM((tiles, outer_rows, tile), jnp.float32),
            pltpu.SemaphoreType.DMA((2,)),
            pltpu.SemaphoreType.DMA((4, tiles)),
            pltpu.SemaphoreType.DMA(pair),
            pltpu.SemaphoreType.DMA(pair),
            pltpu.SemaphoreType.DMA(pair),
            pltpu.SemaphoreType.DMA(pair),
            pltpu.SemaphoreType.DMA((tiles,)),
            pltpu.SemaphoreType.DMA((tiles, GROUP - 1)),
            pltpu.SemaphoreType.DMA((tiles, GROUP - 1)),
        ],
        compiler_params=pltpu.CompilerParams(
            vmem_limit_bytes=VMEM_BYTES, collective_id=1, has_side_effects=True
        ),
        cost_estimate=pl.CostEstimate(
            flops=2 * frame_count * W * states,
            bytes_accessed=2 * frame_count * (states + W),
            transcendentals=0,
        ),
        name="counts",
    )(lead, scale, member)


def segment_of(positions, starts):
    return jnp.sum((starts[:, None] <= positions[None, :]).astype(jnp.int32), axis=0)


def shards(frames, centers, starts):
    devices = lax.axis_size("frames")
    outers = devices // 16
    outer, row, _ = placed(lax.axis_index("frames"))
    groups = [[device_at(o, r, p) for p in range(GROUP)] for o in range(outers) for r in (0, 1)]

    source = centers[:W]
    if lax.axis_size("centers") > 1:
        mine = lax.axis_index("centers") == 0
        source = lax.psum(jnp.where(mine, source, jnp.zeros_like(source)), "centers")
    source = source.reshape(outers, 2, 2, -1, source.shape[1]).transpose(2, 0, 1, 3, 4)
    source = source.reshape(W, -1)

    member, lead, top, total, lead_top, halo_top, halo_total, halo_lead_top = members(
        frames, centers, source
    )
    group_frames = member.shape[1]
    run = group_frames // 2

    def with_halos(values, halos):
        return jnp.concatenate(
            [halos.reshape(2, HALO), values.reshape(2, run)], axis=1
        ).reshape(1, -1)

    def without_halos(values):
        return values.reshape(2, HALO + run)[:, HALO:].reshape(group_frames)

    stats = jnp.concatenate([with_halos(top, halo_top), with_halos(total, halo_total)], axis=0)
    gathered = lax.all_gather(stats, "frames", axis_index_groups=groups)
    all_top = lax.pmax(jnp.max(gathered[:, 0], axis=0), "centers")
    all_total = lax.psum(
        jnp.sum(gathered[:, 1] * jnp.exp2(ALPHA * (gathered[:, 0] - all_top)), axis=0),
        "centers",
    )

    device_frames = frames.shape[0]
    first = jnp.stack([device_at(outer, row, 0), device_at(outer, row, 4)]) * device_frames
    positions = first[:, None] + jnp.arange(-HALO, run, dtype=jnp.int32)[None, :]
    positions = positions.reshape(-1)
    usable = jnp.logical_and(
        segment_of(positions, starts) == segment_of(positions + LAG, starts),
        jnp.logical_and(positions >= 0, positions + LAG < device_frames * devices),
    )
    lead_tops = with_halos(lead_top, halo_lead_top)[0]
    lead_factor = jnp.where(usable, jnp.exp2(ALPHA * (lead_tops - all_top)) / all_total, 0.0)
    lag_factor = jnp.exp2(ALPHA * (with_halos(top, halo_top)[0] - all_top)) / all_total
    moved = lead_factor.reshape(2, HALO + run)[:, HALO - LAG : HALO - LAG + run]
    scale = moved.reshape(group_frames) * without_halos(lag_factor)
    return counts_of(lead, scale[None, :], member, outers)


def solution(mesh):
    return jax.shard_map(
        shards,
        mesh=mesh,
        in_specs=(P("frames", None), P("centers", None), P()),
        out_specs=P("frames", "centers"),
        check_vma=False,
    )
```
